32 devices in a mesh: fsdp: 8 (over z, core), expert: 4 (over y, x).
Axes of the slice: x: 2, y: 2, z: 4, core: 2. Of those that a mesh axis runs over, the one named last changes fastest.
Arguments:
- tokens: bfloat16 [2, 2048, 1024], P(None, ('fsdp', 'expert')), may hold values from -6 to 6
- segments: int32 [2, 32, 64], P(None, ('fsdp', 'expert')), may hold values from 0 to 3, never falling along the last dimension, each value on 1 to 32 neighbouring positions
- routes: int32 [2, 2048, 8], P(None, ('fsdp', 'expert')), may hold values from 0 to 15, all different within a row; in each aligned block of 64 rows (0 to 63, 64 to 127, ..., all dimensions but the last counted through in order) at most 36 rows name the same one
- cotangent: bfloat16 [2, 2048, 1024], P(None, ('fsdp', 'expert')), may hold values from -6 to 6
- gain_attn: bfloat16 [1024], P(('fsdp', 'expert')), may hold values from 0.5 to 1.5
- w_query: bfloat16 [1024, 1024], P(('fsdp', 'expert')), may hold values from -0.1875 to 0.1875
- w_key: bfloat16 [1024, 512], P(('fsdp', 'expert')), may hold values from -0.1875 to 0.1875
- w_value: bfloat16 [1024, 512], P(('fsdp', 'expert')), may hold values from -0.1875 to 0.1875
- w_out: bfloat16 [1024, 1024], P(('fsdp', 'expert')), may hold values from -0.5 to 0.5
- gain_moe: bfloat16 [1024], P(('fsdp', 'expert')), may hold values from 0.5 to 1.5
- w_router: bfloat16 [1024, 16], P(('fsdp', 'expert')), may hold values from -0.09375 to 0.09375
- expert_gate: bfloat16 [16, 1024, 512], P('expert', 'fsdp'), may hold values from -0.1875 to 0.1875
- expert_up: bfloat16 [16, 1024, 512], P('expert', 'fsdp'), may hold values from -0.1875 to 0.1875
- expert_down: bfloat16 [16, 1024, 512], P('expert', 'fsdp'), may hold values from -0.75 to 0.75
Outputs:
- result: bfloat16 [2, 2048, 1024], P(None, ('fsdp', 'expert'))
- grad_tokens: float32 [2, 2048, 1024], P(None, ('fsdp', 'expert'))
- grad_gain_attn: float32 [1024], P(('fsdp', 'expert'))
- grad_w_query: float32 [1024, 1024], P(('fsdp', 'expert'))
- grad_w_key: float32 [1024, 512], P(('fsdp', 'expert'))
- grad_w_value: float32 [1024, 512], P(('fsdp', 'expert'))
- grad_w_out: float32 [1024, 1024], P(('fsdp', 'expert'))
- grad_gain_moe: float32 [1024], P(('fsdp', 'expert'))
- grad_w_router: float32 [1024, 16], P(('fsdp', 'expert'))
- grad_expert_gate: float32 [16, 1024, 512], P('expert', 'fsdp')
- grad_expert_up: float32 [16, 1024, 512], P('expert', 'fsdp')
- grad_expert_down: float32 [16, 1024, 512], P('expert', 'fsdp')
The draws below stay inside these ranges and needn't reach their ends.
Inputs may be any that keep to these rules, and one draw needn't show every extreme that they name: `routes`: each row names 8 different experts; within the tokens of one sequence no expert is named more than 36 times. `segments`: within a sequence the numbers never fall; each document holds 1 to 32 tokens.
All inputs are finite; a program needn't handle non-finite values.
Results may differ from the reference program's by a relative error of at most 0.015.
Values may be sent and summed in bfloat16 or wider, within the bound.
A program may use at most 128 MiB of HBM per device.

```python
import math
import jax
import jax.numpy as jnp
import numpy as np
from jax import lax

D = 1024
HEADS = 16
KV_HEADS = 8
HEAD_DIM = 64
EXPERTS = 16
TOP = 8
FF = 512
SEQ = 64
MICRO = 2
CAP = 36
SEQS = 32
TOKENS = 2048


def level_of(stream_key, extent, split, least, high):
    def one(dim, shards_of):
        steps = jax.random.uniform(jax.random.fold_in(jax.random.fold_in(stream_key, 6), dim), (shards_of,), jnp.float32, least / len(split), high / len(split))
        return jnp.repeat(jnp.exp(steps), extent[dim] // shards_of).reshape((-1,) + (1,) * (len(extent) - dim - 1))

    factor_of = one(*split[0])
    for cut in split[1:]:
        factor_of = factor_of * one(*cut)
    return factor_of


def profile(number_of, total, bound, lean):
    weights = [(1 << 20) // math.isqrt(rank ** lean) + 1 for rank in range(2, number_of + 1)]
    spare, given = total - bound - (number_of - 1), [1] * (number_of - 1)
    while spare > 0:
        candidates = [i for i in range(number_of - 1) if given[i] < bound]
        pool, remaining = sum([weights[i] for i in candidates]), spare
        for i in candidates:
            more = min(bound - given[i], max(1, remaining * weights[i] // pool), spare)
            given[i] = given[i] + more
            spare = spare - more
    return np.array([bound] + given)


def ragged(key, number_of, total, limit, lean):
    if number_of == 2:
        one = jax.random.randint(key, (), max(1, total - limit), min(limit, total - 1) + 1)
        return jnp.stack([one, total - one])
    lengths = jnp.asarray(profile(number_of, total, limit, lean), jnp.int32)
    couples = (number_of - 1) // 2
    source_of, receiver = lengths[1:1 + 2 * couples:2], lengths[2:2 + 2 * couples:2]
    slack = jnp.minimum(source_of - 1, limit - receiver)
    shifted = jax.random.randint(jax.random.fold_in(key, 1), (couples,), 0, 1 << 20) % (slack + 1)
    lengths = lengths.at[1:1 + 2 * couples:2].set(source_of - shifted).at[2:2 + 2 * couples:2].set(receiver + shifted)
    return lengths[jax.random.permutation(jax.random.fold_in(key, 2), number_of)]


def routed_block(own_key, own, number, rows, amount, top, limit, slope):
    sequence = jax.random.permutation(own_key, amount)
    heavy_load, common = shares(amount, rows * top, limit, slope, True), shares(amount, rows * top, limit, slope, False)
    places = jnp.arange(amount)

    def named(sizes, rotation):
        used = int((sizes > 0).sum())
        fixed = max(1, used // 4)
        moved = fixed + (places - fixed + rotation * (used - fixed)) % max(1, amount - fixed)
        return jnp.zeros((amount,), jnp.int32).at[sequence[jnp.where(places < fixed, places, moved)]].set(jnp.asarray(sizes, jnp.int32))

    sizes = jnp.where(number % 4 == 0, named(heavy_load, number // 4), named(common, number - number // 4 - 1))
    mixed = jax.random.permutation(jax.random.fold_in(own, 3), amount)
    donor, sink = mixed[0:amount // 2 * 2:2], mixed[1:amount // 2 * 2:2]
    room = jnp.minimum(sizes[donor] - 1, limit - sizes[sink]) // 2
    room = jnp.where((donor == sequence[0]) | (sink == sequence[0]) | (sizes[sink] == 0), 0, jnp.maximum(room, 0))
    moved = jax.random.randint(jax.random.fold_in(own, 4), (amount // 2,), 0, 1 << 20) % (room + 1)
    sizes = sizes.at[donor].add(-moved).at[sink].add(moved)
    labels = jnp.searchsorted(jnp.cumsum(sizes), jnp.arange(rows * top), side="right").astype(jnp.int32)
    listing = labels.reshape(top, rows).T
    listing = listing[jax.random.permutation(jax.random.fold_in(own, 1), rows)]
    rotation = jax.random.randint(jax.random.fold_in(own, 2), (rows, 1), 0, top)
    return jnp.take_along_axis(listing, (jnp.arange(top)[None, :] + rotation) % top, axis=1)


def shares(count, total, limit, slope, full):
    portions = [(1 << 20) // math.isqrt(rank ** slope) + 1 for rank in range(1, count + 1)]
    largest = limit if full else min(limit, max(-(-total // count), total * portions[0] // sum(portions)))
    least = 1 if total - largest >= count - 1 else 0
    holding, spare = [largest] + [least] * (count - 1), total - largest - least * (count - 1)
    while spare > 0:
        candidates = [i for i in range(1, count) if holding[i] < largest] or [i for i in range(1, count) if holding[i] < limit]
        whole, budget = sum([portions[i] for i in candidates]), spare
        for i in candidates:
            more = min(limit - holding[i], max(1, budget * portions[i] // whole), spare)
            holding[i] = holding[i] + more
            spare = spare - more
    return np.array(holding)


def scatter_about(key, shape, deviation, bound, cuts=(), held_as=jnp.bfloat16):
    drawn = deviation * jax.random.normal(key, shape, jnp.float32)
    if cuts:
        drawn = drawn * level_of(key, shape, cuts, -0.22, 0.18)
    return jnp.clip(drawn, -bound, bound).astype(held_as)


def setup_inputs(seed: int = 0) -> dict:
    arg_keys = jax.random.split(jax.random.key(seed), 15)
    tokens = scatter_about(arg_keys[0], (MICRO, TOKENS, D), 1.0, 6.0, ((1, 32),))
    segments = jax.vmap(lambda own: jnp.searchsorted(jnp.cumsum(ragged(own, 4, SEQ, SEQ // 2, 1)), jnp.arange(SEQ), side="right"))(jax.random.split(arg_keys[1], MICRO * SEQS)).reshape((MICRO, SEQS, SEQ)).astype(jnp.int32)
    routes_keys = jax.random.split(jax.random.fold_in(arg_keys[2], 1), MICRO * TOKENS // SEQ)
    routes_turns = jax.random.permutation(jax.random.fold_in(arg_keys[2], 3), MICRO * TOKENS // SEQ)
    routes = jax.vmap(lambda own, number: routed_block(jax.random.fold_in(arg_keys[2], 2), own, number, SEQ, EXPERTS, TOP, CAP, 0))(routes_keys, routes_turns).reshape((MICRO, TOKENS, TOP))
    cotangent = scatter_about(arg_keys[3], (MICRO, TOKENS, D), 1.0, 6.0, ((1, 32),))
    gain_attn = jnp.clip(1.0 + 0.1 * jax.random.normal(arg_keys[4], (D,), jnp.float32), 0.5, 1.5).astype(jnp.bfloat16)
    w_query = scatter_about(arg_keys[5], (D, HEADS * HEAD_DIM), D ** -0.5, 0.1875, ((0, 32),))
    w_key = scatter_about(arg_keys[6], (D, KV_HEADS * HEAD_DIM), D ** -0.5, 0.1875, ((0, 32),))
    w_value = scatter_about(arg_keys[7], (D, KV_HEADS * HEAD_DIM), D ** -0.5, 0.1875, ((0, 32),))
    w_out = scatter_about(arg_keys[8], (HEADS * HEAD_DIM, D), (HEADS * HEAD_DIM // 8) ** -0.5, 0.5, ((0, 32),))
    gain_moe = jnp.clip(1.0 + 0.1 * jax.random.normal(arg_keys[9], (D,), jnp.float32), 0.5, 1.5).astype(jnp.bfloat16)
    w_router = scatter_about(arg_keys[10], (D, EXPERTS), (4 * D) ** -0.5, 0.09375, ((0, 32),))
    expert_gate = scatter_about(arg_keys[11], (EXPERTS, D, FF), D ** -0.5, 0.1875, ((0, 4), (1, 8)))
    expert_up = scatter_about(arg_keys[12], (EXPERTS, D, FF), D ** -0.5, 0.1875, ((0, 4), (1, 8)))
    expert_down = scatter_about(arg_keys[13], (EXPERTS, D, FF), (FF // 8) ** -0.5, 0.75, ((0, 4), (1, 8)))
    return {"tokens": tokens, "segments": segments, "routes": routes, "cotangent": cotangent, "gain_attn": gain_attn, "w_query": w_query, "w_key": w_key, "w_value": w_value, "w_out": w_out, "gain_moe": gain_moe, "w_router": w_router, "expert_gate": expert_gate, "expert_up": expert_up, "expert_down": expert_down}


@jax.custom_vjp
def low(v):
    return lax.optimization_barrier(v.astype(jnp.bfloat16)).astype(jnp.float32)

@jax.custom_vjp
def low_back(v):
    return v

def low_keep(v):
    return (low(v), None)

def low_pass(kept, grad):
    return (grad,)

def back_keep(v):
    return (v, None)

def back_low(kept, grad):
    return (low(grad),)
low.defvjp(low_keep, low_pass)
low_back.defvjp(back_keep, back_low)
EPS = 1e-06

def both(values):
    return low_back(low(values))

def root_mean(values, gain):
    return values * lax.rsqrt(lax.optimization_barrier(jnp.mean(values * values, -1, keepdims=True)) + EPS) * gain

def rotate(values, direction):
    half = HEAD_DIM // 2
    places = jnp.arange(values.shape[0], dtype=jnp.float32)
    rates = 10000.0 ** (-jnp.arange(half, dtype=jnp.float32) * 2.0 / HEAD_DIM)
    angle = places[:, None] * rates[None, :]
    cosine = jnp.cos(angle)[:, None, :]
    sine = direction * jnp.sin(angle)[:, None, :]
    first = values[..., :half]
    second = values[..., half:]
    return jnp.concatenate([first * cosine - second * sine, second * cosine + first * sine], -1)

def slot_table(route):
    flat = route.reshape(-1)
    hits = (flat[:, None] == jnp.arange(EXPERTS, dtype=jnp.int32)[None, :]).astype(jnp.int32)
    before = jnp.cumsum(hits, axis=0) - hits
    position = lax.optimization_barrier(jnp.sum(before * hits, axis=1))
    slot = flat * CAP + position
    table = (slot[:, None] == jnp.arange(EXPERTS * CAP, dtype=jnp.int32)[None, :]).astype(jnp.float32)
    return table.reshape(route.shape[0], route.shape[1], EXPERTS * CAP)

def sequence_layer(params, source, segment, route):
    gain_attn, w_query, w_key, w_value, w_out, gain_moe, w_router, expert_gate, expert_up, expert_down = params
    highest = lax.Precision.HIGHEST
    length = source.shape[0]
    repeat = HEADS // KV_HEADS
    first_in = low(root_mean(source, gain_attn))
    query_pre = low_back(jnp.dot(first_in, w_query, precision=highest))
    key_pre = low_back(jnp.dot(first_in, w_key, precision=highest))
    query = low(rotate(query_pre.reshape(length, HEADS, HEAD_DIM), 1.0))
    key = low(rotate(key_pre.reshape(length, KV_HEADS, HEAD_DIM), 1.0))
    value = both(jnp.dot(first_in, w_value, precision=highest)).reshape(length, KV_HEADS, HEAD_DIM)
    query = query.reshape(length, KV_HEADS, repeat, HEAD_DIM)
    scores = low_back(jnp.einsum('sgrd,tgd->grst', query, key, precision=highest) * HEAD_DIM ** (-0.5))
    places = jnp.arange(length, dtype=jnp.int32)
    allowed = (places[:, None] >= places[None, :]) & (segment[:, None] == segment[None, :])
    scores = jnp.where(allowed[None, None], scores, -1e+30)
    probs = low(jax.nn.softmax(scores, axis=-1))
    context = jnp.einsum('grst,tgd->sgrd', probs, value, precision=highest).reshape(length, HEADS * HEAD_DIM)
    context = both(context)
    mixed = source + low_back(jnp.dot(context, w_out, precision=highest))
    second_in = low(root_mean(mixed, gain_moe))
    logits = jnp.dot(second_in, w_router, precision=highest)
    chosen = jnp.take_along_axis(logits, route, axis=1)
    gates = jax.nn.softmax(chosen, axis=-1)
    table = slot_table(route)
    place = lax.optimization_barrier(jnp.sum(table, 1))
    combine = lax.optimization_barrier(jnp.sum(gates[:, :, None] * table, 1))
    inputs = low_back(jnp.dot(place.T, second_in, precision=highest)).reshape(EXPERTS, CAP, D)
    gate = low_back(jnp.einsum('erd,edf->erf', inputs, expert_gate, precision=highest))
    up = low_back(jnp.einsum('erd,edf->erf', inputs, expert_up, precision=highest))
    hidden = low(jax.nn.silu(gate) * up)
    produced = both(jnp.einsum('erf,edf->erd', hidden, expert_down, precision=highest)).reshape(EXPERTS * CAP, D)
    return mixed + jnp.dot(combine, produced, precision=highest)

def reference(tokens, segments, routes, cotangent, gain_attn, w_query, w_key, w_value, w_out, gain_moe, w_router, expert_gate, expert_up, expert_down):
    params = tuple((w.astype(jnp.float32) for w in (gain_attn, w_query, w_key, w_value, w_out, gain_moe, w_router, expert_gate, expert_up, expert_down)))
    group = math.gcd(SEQS, max(1, 4096 // SEQ))
    count = MICRO * SEQS // group
    source_all = tokens.astype(jnp.float32).reshape(count, group, SEQ, D)
    upstream_all = cotangent.astype(jnp.float32).reshape(count, group, SEQ, D)
    segment_all = segments.reshape(count, group, SEQ)
    route_all = routes.reshape(count, group, SEQ, TOP)

    def one_group(totals, item):
        source, segment, route, upstream = item

        def forward(weights, values):
            return jax.vmap(sequence_layer, in_axes=(None, 0, 0, 0))(weights, values, segment, route)
        output, pull = jax.vjp(forward, params, source)
        weight_grads, source_grad = pull(upstream)
        totals = tuple((a + b for a, b in zip(totals, weight_grads)))
        return (totals, (output.astype(jnp.bfloat16), source_grad))
    start = tuple((jnp.zeros(p.shape, jnp.float32) for p in params))
    totals, (outputs, source_grads) = lax.scan(one_group, start, (source_all, segment_all, route_all, upstream_all))
    result = outputs.reshape(MICRO, TOKENS, D)
    grad_tokens = source_grads.reshape(MICRO, TOKENS, D)
    return (result, grad_tokens, totals[0], totals[1], totals[2], totals[3], totals[4], totals[5], totals[6], totals[7], totals[8], totals[9])
```

```python
import jax
import jax.numpy as jnp
import numpy as np
from jax import lax
from jax.sharding import PartitionSpec as P

HEADS = 16
KV_HEADS = 8
HEAD_DIM = 64
EXPERTS = 16
TOP = 8


EPS = 1e-06


def norm_back(grad, values, inverse, gain):
    unit = values * inverse
    scaled = grad * gain
    back = inverse * (scaled - unit * jnp.mean(scaled * unit, -1, keepdims=True))
    return (back, jnp.sum(grad * unit, 0))


def turn_tables(rows, length):
    half = HEAD_DIM // 2
    places = (np.arange(rows) % length).astype(np.float64)
    rates = 10000.0 ** (-np.arange(half, dtype=np.float64) * 2.0 / HEAD_DIM)
    angle = places[:, None] * rates[None, :]
    return (
        np.cos(angle).astype(np.float32)[:, None, :],
        np.sin(angle).astype(np.float32)[:, None, :],
    )


def rotate(values, cosine, sine):
    half = HEAD_DIM // 2
    first = values[..., :half]
    second = values[..., half:]
    return jnp.concatenate([first * cosine - second * sine, second * cosine + first * sine], -1)


def product(left, right):
    return jnp.dot(left, right, preferred_element_type=jnp.float32)


def inner(left, right):
    return lax.dot_general(
        left, right, (((0,), (0,)), ((), ())), preferred_element_type=jnp.float32
    )


def outer_back(left, right):
    return lax.dot_general(
        left, right, (((1,), (1,)), ((), ())), preferred_element_type=jnp.float32
    )


def per_device(
    tokens,
    segments,
    routes,
    cotangent,
    gain_attn,
    w_query,
    w_key,
    w_value,
    w_out,
    gain_moe,
    w_router,
    expert_gate,
    expert_up,
    expert_down,
):
    micro, length, width = tokens.shape
    rows = micro * length
    hidden_units = expert_gate.shape[2]
    repeat = HEADS // KV_HEADS
    scale = HEAD_DIM ** (-0.5)
    highest = lax.Precision.HIGHEST
    bf16 = jnp.bfloat16
    f32 = jnp.float32
    n_fsdp = lax.axis_size("fsdp")
    n_expert = lax.axis_size("expert")
    local = expert_gate.shape[0]
    own = w_query.shape[0]
    wide_q = HEADS * HEAD_DIM
    wide_k = KV_HEADS * HEAD_DIM
    wide_qkv = wide_q + 2 * wide_k

    n_chip = n_fsdp // 2
    same_core = [[2 * chip + core for chip in range(n_chip)] for core in range(2)]
    other_core = [(index, index ^ 1) for index in range(n_fsdp)]
    first_core = lax.axis_index("fsdp") % 2 == 0

    def across(block, axis, groups=None):
        return lax.all_to_all(
            block, axis, split_axis=0, concat_axis=0, axis_index_groups=groups, tiled=True
        )

    def spread_out(block, axis, groups=None):
        count = lax.axis_size(axis) if groups is None else len(groups[0])
        copies = jnp.broadcast_to(block[None], (count,) + block.shape)
        copies = copies.reshape((count * block.shape[0],) + block.shape[1:])
        return across(copies, axis, groups)

    def columns_of(block):
        return block.transpose(1, 0, 2).reshape(block.shape[1], local * hidden_units)

    experts = lax.all_gather(
        jnp.concatenate(
            [columns_of(expert_gate), columns_of(expert_up), columns_of(expert_down)], 1
        ),
        "fsdp",
        axis=0,
        tiled=True,
    )
    units = local * hidden_units
    pair_weight = experts[:, : 2 * units]
    down_weight = experts[:, 2 * units :]

    packed = jnp.concatenate(
        [
            w_query,
            w_key,
            w_value,
            w_router,
            gain_attn[:, None],
            gain_moe[:, None],
            jnp.zeros((own, 128 - EXPERTS - 2), bf16),
            w_out,
        ],
        1,
    )
    part = spread_out(packed, "fsdp", same_core)

    def whole_of(block):
        mine = spread_out(block, "expert")
        other = lax.ppermute(mine, "fsdp", other_core)
        both = jnp.stack(
            [jnp.where(first_core, mine, other), jnp.where(first_core, other, mine)]
        )
        return (
            both.reshape(2, n_expert, n_chip, own, block.shape[1])
            .transpose(2, 0, 1, 3, 4)
            .reshape(width, block.shape[1])
        )

    front = whole_of(part[:, : wide_qkv + 128])
    out_weight = whole_of(part[:, wide_qkv + 128 :])
    qkv_weight = front[:, :wide_qkv]
    small = front[:, wide_qkv:]
    router_weight = small[:, :EXPERTS]
    gains = small[:, EXPERTS : EXPERTS + 2].astype(f32).T
    first_gain = gains[0]
    second_gain = gains[1]

    source = tokens.reshape(rows, width).astype(f32)
    first_inverse = lax.rsqrt(jnp.mean(source * source, -1, keepdims=True) + EPS)
    first_in = (source * first_inverse * first_gain).astype(bf16)
    segment = segments.reshape(rows)
    places = jnp.arange(rows, dtype=jnp.int32)
    same = (places[:, None] // length) == (places[None, :] // length)
    allowed = (
        same & (places[:, None] >= places[None, :]) & (segment[:, None] == segment[None, :])
    )
    cosine, sine = turn_tables(rows, length)
    qkv = product(first_in, qkv_weight)
    query = rotate(qkv[:, :wide_q].reshape(rows, HEADS, HEAD_DIM), cosine, sine)
    query = query.astype(bf16).reshape(rows, KV_HEADS, repeat, HEAD_DIM)
    key = rotate(
        qkv[:, wide_q : wide_q + wide_k].reshape(rows, KV_HEADS, HEAD_DIM), cosine, sine
    ).astype(bf16)
    value = qkv[:, wide_q + wide_k :].astype(bf16).reshape(rows, KV_HEADS, HEAD_DIM)
    scores = (
        jnp.einsum("sgrd,tgd->grst", query, key, preferred_element_type=f32) * scale
    )
    scores = jnp.where(allowed[None, None], scores, -1e30)
    peak = jnp.max(scores, -1, keepdims=True)
    raised = jnp.exp(scores - peak)
    probs = raised / jnp.sum(raised, -1, keepdims=True)
    probs_kept = probs.astype(bf16)
    context = jnp.einsum("grst,tgd->sgrd", probs_kept, value, preferred_element_type=f32)
    context = context.reshape(rows, wide_q).astype(bf16)
    mixed = source + product(context, out_weight)
    second_inverse = lax.rsqrt(jnp.mean(mixed * mixed, -1, keepdims=True) + EPS)
    second_in = (mixed * second_inverse * second_gain).astype(bf16)

    route = routes.reshape(rows, TOP)
    expert_ids = jnp.arange(EXPERTS, dtype=jnp.int32)
    chosen = jnp.any(route[:, :, None] == expert_ids[None, None, :], 1)
    logits = product(second_in, router_weight)
    top = jnp.max(jnp.where(chosen, logits, -jnp.inf), -1, keepdims=True)
    weight = jnp.where(chosen, jnp.exp(jnp.where(chosen, logits - top, 0.0)), 0.0)
    gates = weight / jnp.sum(weight, -1, keepdims=True)

    def halves(block):
        high = block.astype(bf16)
        return [high, (block - high.astype(f32)).astype(bf16)]

    upstream_kept = cotangent.reshape(rows, width)
    upstream = upstream_kept.astype(f32)
    upstream_all = spread_out(upstream_kept, "expert")
    gates_out = gates.reshape(rows, n_expert, local).transpose(1, 0, 2)
    sent = jnp.concatenate(
        [jnp.broadcast_to(second_in[None], (n_expert, rows, width))]
        + halves(gates_out)
        + [jnp.zeros((n_expert, rows, 128 - 2 * local), bf16)],
        2,
    ).reshape(n_expert * rows, width + 128)
    arrived = lax.all_to_all(sent, "expert", split_axis=0, concat_axis=0, tiled=True)
    tokens_all = arrived[:, :width]
    gates_all = arrived[:, width : width + local].astype(f32) + arrived[
        :, width + local : width + 2 * local
    ].astype(f32)
    count = n_expert * rows
    lane_expert = lax.broadcasted_iota(jnp.int32, (1, units), 1) // hidden_units
    gates_wide = gates_all[:, :1]
    for index in range(1, local):
        gates_wide = jnp.where(lane_expert == index, gates_all[:, index : index + 1], gates_wide)

    pair = product(tokens_all, pair_weight)
    gate = pair[:, :units]
    up = pair[:, units:]
    sigma = jax.nn.sigmoid(gate)
    silu = gate * sigma
    hidden = silu * up
    hidden_gated = (hidden * gates_wide).astype(bf16)
    returned = lax.all_to_all(
        outer_back(hidden_gated, down_weight).astype(bf16),
        "expert",
        split_axis=0,
        concat_axis=0,
        tiled=True,
    )
    down_total = inner(upstream_all, hidden_gated).astype(bf16)
    down_part = lax.psum_scatter(down_total, "fsdp", scatter_dimension=0, tiled=True)
    hidden_raw = product(upstream_all, down_weight)
    meeting = hidden_raw * hidden
    gate_grad_all = jnp.concatenate(
        [
            jnp.sum(
                meeting[:, index * hidden_units : (index + 1) * hidden_units], 1, keepdims=True
            )
            for index in range(local)
        ],
        1,
    )
    hidden_grad = hidden_raw * gates_wide
    gate_back = (hidden_grad * up * sigma * (1.0 + gate * (1.0 - sigma))).astype(bf16)
    up_back = (hidden_grad * silu).astype(bf16)
    pair_back = jnp.concatenate([gate_back, up_back], 1)
    sent_back = jnp.concatenate(
        [outer_back(pair_back, pair_weight).astype(bf16)]
        + halves(gate_grad_all)
        + [jnp.zeros((count, 128 - 2 * local), bf16)],
        1,
    )
    home = lax.all_to_all(sent_back, "expert", split_axis=0, concat_axis=0, tiled=True)
    pair_total = inner(tokens_all, pair_back).astype(bf16)
    home, pair_total = lax.optimization_barrier((home, pair_total))
    pair_part = lax.psum_scatter(pair_total, "fsdp", scatter_dimension=0, tiled=True)

    result = mixed + jnp.sum(returned.reshape(n_expert, rows, width).astype(f32), 0)
    home = home.reshape(n_expert, rows, width + 128).astype(f32)
    gate_grad = home[:, :, width : width + local] + home[:, :, width + local : width + 2 * local]
    gate_grad = gate_grad.transpose(1, 0, 2).reshape(rows, EXPERTS)
    logit_grad = gates * (gate_grad - jnp.sum(gates * gate_grad, -1, keepdims=True))
    router_in_grad = jnp.dot(logit_grad, router_weight.astype(f32).T, precision=highest)
    second_grad = jnp.sum(home[:, :, :width], 0) + router_in_grad
    mixed_back, second_gain_grad = norm_back(second_grad, mixed, second_inverse, second_gain)
    mixed_grad = upstream + mixed_back
    branch_grad = mixed_grad.astype(bf16)
    grad_router = lax.dot_general(
        second_in.astype(f32), logit_grad, (((0,), (0,)), ((), ())), precision=highest
    )

    def to_owners(parts):
        kept = []
        given = []
        for block in parts:
            wide = block.shape[1]
            split = block.astype(bf16).reshape(n_chip, 2, n_expert, own, wide)
            split = split.transpose(1, 2, 0, 3, 4).reshape(2, width // 2, wide)
            kept.append(jnp.where(first_core, split[0], split[1]))
            given.append(jnp.where(first_core, split[1], split[0]))
        kept = jnp.concatenate(kept, 1)
        taken = lax.ppermute(jnp.concatenate(given, 1), "fsdp", other_core)
        pieces = across((kept.astype(f32) + taken.astype(f32)).astype(bf16), "expert")
        pieces = pieces.reshape(n_expert, n_chip * own, -1).astype(f32)
        return jnp.sum(pieces, 0).astype(bf16)

    out_pieces = to_owners(
        [
            inner(context, branch_grad),
            jnp.concatenate(
                [
                    grad_router,
                    second_gain_grad[:, None],
                    jnp.zeros((width, 128 - EXPERTS - 1), f32),
                ],
                1,
            ),
        ]
    )
    context_grad = (
        outer_back(branch_grad, out_weight)
        .astype(bf16)
        .reshape(rows, KV_HEADS, repeat, HEAD_DIM)
    )
    value_grad = jnp.einsum(
        "grst,sgrd->tgd", probs_kept, context_grad, preferred_element_type=f32
    )
    value_grad = value_grad.astype(bf16).reshape(rows, wide_k)
    prob_grad = jnp.einsum("sgrd,tgd->grst", context_grad, value, preferred_element_type=f32)
    score_grad = (
        probs * (prob_grad - jnp.sum(probs * prob_grad, -1, keepdims=True))
    ).astype(bf16)
    query_grad = (
        jnp.einsum("grst,tgd->sgrd", score_grad, key, preferred_element_type=f32) * scale
    )
    key_grad = (
        jnp.einsum("grst,sgrd->tgd", score_grad, query, preferred_element_type=f32) * scale
    )
    query_pre_grad = (
        rotate(query_grad.reshape(rows, HEADS, HEAD_DIM), cosine, -sine)
        .astype(bf16)
        .reshape(rows, wide_q)
    )
    key_pre_grad = rotate(key_grad, cosine, -sine).astype(bf16).reshape(rows, wide_k)
    qkv_grad = jnp.concatenate([query_pre_grad, key_pre_grad, value_grad], 1)
    first_grad = outer_back(qkv_grad, qkv_weight)
    source_back, first_gain_grad = norm_back(first_grad, source, first_inverse, first_gain)
    grad_tokens = mixed_grad + source_back
    qkv_pieces = to_owners(
        [
            inner(first_in, qkv_grad),
            jnp.concatenate([first_gain_grad[:, None], jnp.zeros((width, 127), f32)], 1),
        ]
    )
    dense_pieces = across(jnp.concatenate([qkv_pieces, out_pieces], 1), "fsdp", same_core)
    dense_part = jnp.sum(dense_pieces.reshape(n_chip, own, -1).astype(f32), 0)

    def experts_of(block):
        return (
            block.reshape(block.shape[0], local, hidden_units).transpose(1, 0, 2).astype(f32)
        )

    after = wide_qkv + 128
    return (
        result.astype(bf16).reshape(micro, length, width),
        grad_tokens.reshape(micro, length, width),
        dense_part[:, wide_qkv],
        dense_part[:, :wide_q],
        dense_part[:, wide_q : wide_q + wide_k],
        dense_part[:, wide_q + wide_k : wide_qkv],
        dense_part[:, after : after + width],
        dense_part[:, after + width + EXPERTS],
        dense_part[:, after + width : after + width + EXPERTS],
        experts_of(pair_part[:, :units]),
        experts_of(pair_part[:, units:]),
        experts_of(down_part),
    )


def solution(mesh):
    placed = (
        P(None, ("fsdp", "expert"), None),
        P(None, ("fsdp", "expert"), None),
        P(None, ("fsdp", "expert"), None),
        P(None, ("fsdp", "expert"), None),
        P(("fsdp", "expert")),
        P(("fsdp", "expert"), None),
        P(("fsdp", "expert"), None),
        P(("fsdp", "expert"), None),
        P(("fsdp", "expert"), None),
        P(("fsdp", "expert")),
        P(("fsdp", "expert"), None),
        P("expert", "fsdp", None),
        P("expert", "fsdp", None),
        P("expert", "fsdp", None),
    )
    return jax.shard_map(
        per_device,
        mesh=mesh,
        in_specs=placed,
        out_specs=(
            P(None, ("fsdp", "expert"), None),
            P(None, ("fsdp", "expert"), None),
            P(("fsdp", "expert")),
            P(("fsdp", "expert"), None),
            P(("fsdp", "expert"), None),
            P(("fsdp", "expert"), None),
            P(("fsdp", "expert"), None),
            P(("fsdp", "expert")),
            P(("fsdp", "expert"), None),
            P("expert", "fsdp", None),
            P("expert", "fsdp", None),
            P("expert", "fsdp", None),
        ),
        check_vma=False,
    )
```

```python
import functools

import jax
import jax.numpy as jnp
import numpy as np
from jax import lax
from jax.experimental import pallas as pl
from jax.experimental.pallas import tpu as pltpu
from jax.sharding import PartitionSpec as P

HEADS = 16
KV_HEADS = 8
HEAD_DIM = 64
EXPERTS = 16
TOP = 8


EPS = 1e-06


def norm_back(grad, values, inverse, gain):
    unit = values * inverse
    scaled = grad * gain
    back = inverse * (scaled - unit * jnp.mean(scaled * unit, -1, keepdims=True))
    return (back, jnp.sum(grad * unit, 0))


def turn_tables(rows, length):
    half = HEAD_DIM // 2
    places = (np.arange(rows) % length).astype(np.float64)
    rates = 10000.0 ** (-np.arange(half, dtype=np.float64) * 2.0 / HEAD_DIM)
    angle = places[:, None] * rates[None, :]
    return (
        np.cos(angle).astype(np.float32)[:, None, :],
        np.sin(angle).astype(np.float32)[:, None, :],
    )


def rotate(values, cosine, sine):
    half = HEAD_DIM // 2
    first = values[..., :half]
    second = values[..., half:]
    return jnp.concatenate([first * cosine - second * sine, second * cosine + first * sine], -1)


def product(left, right):
    return jnp.dot(left, right, preferred_element_type=jnp.float32)


def inner(left, right):
    return lax.dot_general(
        left, right, (((0,), (0,)), ((), ())), preferred_element_type=jnp.float32
    )


def outer_back(left, right):
    return lax.dot_general(
        left, right, (((1,), (1,)), ((), ())), preferred_element_type=jnp.float32
    )


def one_expert(x, u, x_turned, u_turned, weight, gate_column):
    unit = weight.shape[1] // 3
    w_gate = weight[:, :unit]
    w_up = weight[:, unit : 2 * unit]
    w_down = weight[:, 2 * unit :]
    gate = product(x, w_gate)
    up = product(x, w_up)
    raw = product(u, w_down)
    sigma = 1.0 / (1.0 + jnp.exp(-gate))
    silu = gate * sigma
    hidden = silu * up
    gate_grad = jnp.sum(raw * hidden, 1, keepdims=True)
    gated = (hidden * gate_column).astype(jnp.bfloat16)
    back = raw * gate_column
    gate_back = (back * up * (sigma + silu * (1.0 - sigma))).astype(jnp.bfloat16)
    up_back = (back * silu).astype(jnp.bfloat16)
    return (
        outer_back(gated, w_down),
        outer_back(gate_back, w_gate) + outer_back(up_back, w_up),
        gate_grad,
        product(x_turned, gate_back).astype(jnp.bfloat16),
        product(x_turned, up_back).astype(jnp.bfloat16),
        product(u_turned, gated).astype(jnp.bfloat16),
    )


def pick_gate(block, expert):
    lane = lax.broadcasted_iota(jnp.int32, block.shape, 1)
    mine = (lane == expert) | (lane == expert + EXPERTS)
    return mine, jnp.sum(jnp.where(mine, block, 0.0), 1, keepdims=True)


def both_halves(total):
    lane = lax.broadcasted_iota(jnp.int32, total.shape, 1)
    high = total.astype(jnp.bfloat16).astype(jnp.float32)
    return jnp.where(lane < EXPERTS, high, total - high).astype(jnp.bfloat16)


def experts_kernel(
    local, x, gates, u, weight, returned, back, totals, sum_out, sum_back, sum_gate, x_turned, u_turned
):
    step = pl.program_id(0)
    width = x.shape[1]

    @pl.when(step == 0)
    def _():
        x_turned[...] = x[...].T
        u_turned[...] = u[...].T
        sum_out[...] = jnp.zeros_like(sum_out)
        sum_back[...] = jnp.zeros_like(sum_back)
        sum_gate[...] = jnp.zeros_like(sum_gate)

    expert = lax.axis_index("expert") * local + step
    mine, gate_column = pick_gate(gates[...].astype(jnp.float32), expert)
    out, token_back, gate_grad, gate_total, up_total, down_total = one_expert(
        x[...], u[...], x_turned[...], u_turned[...], weight[...], gate_column
    )
    unit = weight.shape[1] // 3
    totals[:, :unit] = gate_total
    totals[:, unit : 2 * unit] = up_total
    totals[:, 2 * unit :] = down_total
    sum_out[...] += out
    sum_back[...] += token_back
    sum_gate[...] += jnp.where(mine, gate_grad, 0.0)

    @pl.when(step == local - 1)
    def _():
        returned[...] = sum_out[...].astype(jnp.bfloat16)
        back[:, :width] = sum_back[...].astype(jnp.bfloat16)
        back[:, width:] = both_halves(sum_gate[...])


def run_experts(arrived, u, weight, local):
    count, width = u.shape
    wide = weight.shape[1] // local
    bf16 = jnp.bfloat16
    if count <= 512:
        return pl.pallas_call(
            functools.partial(experts_kernel, local),
            grid=(local,),
            in_specs=[
                pl.BlockSpec((count, width), lambda step: (0, 0)),
                pl.BlockSpec((count, 128), lambda step: (0, width // 128)),
                pl.BlockSpec((count, width), lambda step: (0, 0)),
                pl.BlockSpec((width, wide), lambda step: (0, step)),
            ],
            out_specs=[
                pl.BlockSpec((count, width), lambda step: (0, 0)),
                pl.BlockSpec((count, width + 128), lambda step: (0, 0)),
                pl.BlockSpec((width, wide), lambda step: (0, step)),
            ],
            out_shape=[
                jax.ShapeDtypeStruct((count, width), bf16),
                jax.ShapeDtypeStruct((count, width + 128), bf16),
                jax.ShapeDtypeStruct(weight.shape, bf16),
            ],
            scratch_shapes=[
                pltpu.VMEM((count, width), jnp.float32),
                pltpu.VMEM((count, width), jnp.float32),
                pltpu.VMEM((count, 128), jnp.float32),
                pltpu.VMEM((width, count), bf16),
                pltpu.VMEM((width, count), bf16),
            ],
            compiler_params=pltpu.CompilerParams(vmem_limit_bytes=48 * 1024 * 1024),
            cost_estimate=pl.CostEstimate(
                flops=6 * count * width * weight.shape[1],
                bytes_accessed=4 * width * weight.shape[1],
                transcendentals=count * weight.shape[1] // 3,
            ),
        )(arrived, arrived, u, weight)
    x = arrived[:, :width]
    gates = arrived[:, width:].astype(jnp.float32)
    sum_out = 0.0
    sum_back = 0.0
    sum_gate = 0.0
    totals = []
    for step in range(local):
        expert = lax.axis_index("expert") * local + step
        mine, gate_column = pick_gate(gates, expert)
        out, token_back, gate_grad, *own_totals = one_expert(
            x, u, x.T, u.T, weight[:, step * wide : (step + 1) * wide], gate_column
        )
        sum_out = sum_out + out
        sum_back = sum_back + token_back
        sum_gate = sum_gate + jnp.where(mine, gate_grad, 0.0)
        totals += own_totals
    back = jnp.concatenate([sum_back.astype(bf16), both_halves(sum_gate)], 1)
    return sum_out.astype(bf16), back, jnp.concatenate(totals, 1)


def per_device(
    tokens,
    segments,
    routes,
    cotangent,
    gain_attn,
    w_query,
    w_key,
    w_value,
    w_out,
    gain_moe,
    w_router,
    expert_gate,
    expert_up,
    expert_down,
):
    micro, length, width = tokens.shape
    rows = micro * length
    hidden_units = expert_gate.shape[2]
    repeat = HEADS // KV_HEADS
    scale = HEAD_DIM ** (-0.5)
    highest = lax.Precision.HIGHEST
    bf16 = jnp.bfloat16
    f32 = jnp.float32
    n_fsdp = lax.axis_size("fsdp")
    n_expert = lax.axis_size("expert")
    local = expert_gate.shape[0]
    own = w_query.shape[0]
    wide_q = HEADS * HEAD_DIM
    wide_k = KV_HEADS * HEAD_DIM
    wide_qkv = wide_q + 2 * wide_k

    n_chip = n_fsdp // 2
    same_core = [[2 * chip + core for chip in range(n_chip)] for core in range(2)]
    other_core = [(index, index ^ 1) for index in range(n_fsdp)]
    first_core = lax.axis_index("fsdp") % 2 == 0

    def across(block, axis, groups=None):
        return lax.all_to_all(
            block, axis, split_axis=0, concat_axis=0, axis_index_groups=groups, tiled=True
        )

    def spread_out(block, axis, groups=None):
        count = lax.axis_size(axis) if groups is None else len(groups[0])
        copies = jnp.broadcast_to(block[None], (count,) + block.shape)
        copies = copies.reshape((count * block.shape[0],) + block.shape[1:])
        return across(copies, axis, groups)

    packed = jnp.concatenate(
        [
            w_query,
            w_key,
            w_value,
            w_router,
            gain_attn[:, None],
            gain_moe[:, None],
            jnp.zeros((own, 128 - EXPERTS - 2), bf16),
            w_out,
        ],
        1,
    )
    part = spread_out(packed, "fsdp", same_core)

    held_gate, held_up, held_down, part = lax.optimization_barrier(
        (expert_gate, expert_up, expert_down, part)
    )
    experts = lax.all_gather(
        jnp.concatenate([held_gate, held_up, held_down], 2)
        .transpose(1, 0, 2)
        .reshape(held_gate.shape[1], 3 * local * hidden_units),
        "fsdp",
        axis=0,
        tiled=True,
    )

    def whole_of(block):
        mine = spread_out(block, "expert")
        other = lax.ppermute(mine, "fsdp", other_core)
        both = jnp.stack(
            [jnp.where(first_core, mine, other), jnp.where(first_core, other, mine)]
        )
        return (
            both.reshape(2, n_expert, n_chip, own, block.shape[1])
            .transpose(2, 0, 1, 3, 4)
            .reshape(width, block.shape[1])
        )

    front = whole_of(part[:, : wide_qkv + 128])
    out_weight = whole_of(part[:, wide_qkv + 128 :])
    qkv_weight = front[:, :wide_qkv]
    small = front[:, wide_qkv:]
    router_weight = small[:, :EXPERTS]
    gains = small[:, EXPERTS : EXPERTS + 2].astype(f32).T
    first_gain = gains[0]
    second_gain = gains[1]

    source = tokens.reshape(rows, width).astype(f32)
    first_inverse = lax.rsqrt(jnp.mean(source * source, -1, keepdims=True) + EPS)
    first_in = (source * first_inverse * first_gain).astype(bf16)
    segment = segments.reshape(rows)
    places = jnp.arange(rows, dtype=jnp.int32)
    same = (places[:, None] // length) == (places[None, :] // length)
    allowed = (
        same & (places[:, None] >= places[None, :]) & (segment[:, None] == segment[None, :])
    )
    cosine, sine = turn_tables(rows, length)
    qkv = product(first_in, qkv_weight)
    query = rotate(qkv[:, :wide_q].reshape(rows, HEADS, HEAD_DIM), cosine, sine)
    query = query.astype(bf16).reshape(rows, KV_HEADS, repeat, HEAD_DIM)
    key = rotate(
        qkv[:, wide_q : wide_q + wide_k].reshape(rows, KV_HEADS, HEAD_DIM), cosine, sine
    ).astype(bf16)
    value = qkv[:, wide_q + wide_k :].astype(bf16).reshape(rows, KV_HEADS, HEAD_DIM)
    scores = (
        jnp.einsum("sgrd,tgd->grst", query, key, preferred_element_type=f32) * scale
    )
    scores = jnp.where(allowed[None, None], scores, -1e30)
    peak = jnp.max(scores, -1, keepdims=True)
    raised = jnp.exp(scores - peak)
    probs = raised / jnp.sum(raised, -1, keepdims=True)
    probs_kept = probs.astype(bf16)
    context = jnp.einsum("grst,tgd->sgrd", probs_kept, value, preferred_element_type=f32)
    context = context.reshape(rows, wide_q).astype(bf16)
    mixed = source + product(context, out_weight)
    second_inverse = lax.rsqrt(jnp.mean(mixed * mixed, -1, keepdims=True) + EPS)
    second_in = (mixed * second_inverse * second_gain).astype(bf16)

    route = routes.reshape(rows, TOP)
    expert_ids = jnp.arange(EXPERTS, dtype=jnp.int32)
    chosen = jnp.any(route[:, :, None] == expert_ids[None, None, :], 1)
    logits = product(second_in, router_weight)
    top = jnp.max(jnp.where(chosen, logits, -jnp.inf), -1, keepdims=True)
    weight = jnp.where(chosen, jnp.exp(jnp.where(chosen, logits - top, 0.0)), 0.0)
    gates = weight / jnp.sum(weight, -1, keepdims=True)

    upstream_kept = cotangent.reshape(rows, width)
    upstream = upstream_kept.astype(f32)
    held_upstream, _ = lax.optimization_barrier((upstream_kept, part))
    upstream_all = spread_out(held_upstream, "expert")
    gates_high = gates.astype(bf16)
    sent = jnp.concatenate(
        [
            second_in,
            gates_high,
            (gates - gates_high.astype(f32)).astype(bf16),
            jnp.zeros((rows, 128 - 2 * EXPERTS), bf16),
        ],
        1,
    )
    sent, upstream_all = lax.optimization_barrier((sent, upstream_all))
    arrived = spread_out(sent, "expert")

    produced, sent_back, expert_total = run_experts(arrived, upstream_all, experts, local)
    home = across(sent_back, "expert")
    expert_part = lax.psum_scatter(expert_total, "fsdp", scatter_dimension=0, tiled=True)

    home = jnp.sum(home.reshape(n_expert, rows, width + 128).astype(f32), 0)
    gate_grad = home[:, width : width + EXPERTS] + home[:, width + EXPERTS : width + 2 * EXPERTS]
    logit_grad = gates * (gate_grad - jnp.sum(gates * gate_grad, -1, keepdims=True))
    router_in_grad = jnp.dot(logit_grad, router_weight.astype(f32).T, precision=highest)
    second_grad = home[:, :width] + router_in_grad
    mixed_back, second_gain_grad = norm_back(second_grad, mixed, second_inverse, second_gain)
    mixed_grad = upstream + mixed_back
    branch_grad = mixed_grad.astype(bf16)
    branch_grad, produced = lax.optimization_barrier((branch_grad, produced))
    returned = across(produced, "expert")
    grad_router = lax.dot_general(
        second_in.astype(f32), logit_grad, (((0,), (0,)), ((), ())), precision=highest
    )

    def to_owners(parts):
        kept = []
        given = []
        for block in parts:
            wide = block.shape[1]
            split = block.astype(bf16).reshape(n_chip, 2, n_expert, own, wide)
            split = split.transpose(1, 2, 0, 3, 4).reshape(2, width // 2, wide)
            kept.append(jnp.where(first_core, split[0], split[1]))
            given.append(jnp.where(first_core, split[1], split[0]))
        kept = jnp.concatenate(kept, 1)
        taken = lax.ppermute(jnp.concatenate(given, 1), "fsdp", other_core)
        return (kept.astype(f32) + taken.astype(f32)).astype(bf16)

    def expert_hop(block):
        pieces = across(block, "expert").reshape(n_expert, n_chip * own, -1)
        return jnp.sum(pieces.astype(f32), 0).astype(bf16)

    out_half = to_owners(
        [
            inner(context, branch_grad),
            jnp.concatenate(
                [
                    grad_router,
                    second_gain_grad[:, None],
                    jnp.zeros((width, 128 - EXPERTS - 1), f32),
                ],
                1,
            ),
        ]
    )
    context_grad = (
        outer_back(branch_grad, out_weight)
        .astype(bf16)
        .reshape(rows, KV_HEADS, repeat, HEAD_DIM)
    )
    value_grad = jnp.einsum(
        "grst,sgrd->tgd", probs_kept, context_grad, preferred_element_type=f32
    )
    value_grad = value_grad.astype(bf16).reshape(rows, wide_k)
    prob_grad = jnp.einsum("sgrd,tgd->grst", context_grad, value, preferred_element_type=f32)
    score_grad = (
        probs * (prob_grad - jnp.sum(probs * prob_grad, -1, keepdims=True))
    ).astype(bf16)
    score_grad, returned = lax.optimization_barrier((score_grad, returned))
    result = mixed + jnp.sum(returned.reshape(n_expert, rows, width).astype(f32), 0)
    query_grad = (
        jnp.einsum("grst,tgd->sgrd", score_grad, key, preferred_element_type=f32) * scale
    )
    key_grad = (
        jnp.einsum("grst,sgrd->tgd", score_grad, query, preferred_element_type=f32) * scale
    )
    query_pre_grad = (
        rotate(query_grad.reshape(rows, HEADS, HEAD_DIM), cosine, -sine)
        .astype(bf16)
        .reshape(rows, wide_q)
    )
    key_pre_grad = rotate(key_grad, cosine, -sine).astype(bf16).reshape(rows, wide_k)
    qkv_grad = jnp.concatenate([query_pre_grad, key_pre_grad, value_grad], 1)
    out_pieces = expert_hop(out_half)
    qkv_grad, out_pieces = lax.optimization_barrier((qkv_grad, out_pieces))
    first_grad = outer_back(qkv_grad, qkv_weight)
    source_back, first_gain_grad = norm_back(first_grad, source, first_inverse, first_gain)
    grad_tokens = mixed_grad + source_back
    qkv_half = to_owners(
        [
            inner(first_in, qkv_grad),
            jnp.concatenate([first_gain_grad[:, None], jnp.zeros((width, 127), f32)], 1),
        ]
    )
    dense_half = jnp.concatenate([expert_hop(qkv_half), out_pieces], 1)
    dense_pieces = across(dense_half, "fsdp", same_core)
    dense_part = jnp.sum(dense_pieces.reshape(n_chip, own, -1).astype(f32), 0)
    qkv_part = dense_part[:, : wide_qkv + 128]
    out_part = dense_part[:, wide_qkv + 128 :]

    expert_part = expert_part.reshape(expert_part.shape[0], local, 3, hidden_units)
    expert_part = expert_part.transpose(2, 1, 0, 3).astype(f32)
    return (
        result.astype(bf16).reshape(micro, length, width),
        grad_tokens.reshape(micro, length, width),
        qkv_part[:, wide_qkv],
        qkv_part[:, :wide_q],
        qkv_part[:, wide_q : wide_q + wide_k],
        qkv_part[:, wide_q + wide_k : wide_qkv],
        out_part[:, :width],
        out_part[:, width + EXPERTS],
        out_part[:, width : width + EXPERTS],
        expert_part[0],
        expert_part[1],
        expert_part[2],
    )


def solution(mesh):
    placed = (
        P(None, ("fsdp", "expert"), None),
        P(None, ("fsdp", "expert"), None),
        P(None, ("fsdp", "expert"), None),
        P(None, ("fsdp", "expert"), None),
        P(("fsdp", "expert")),
        P(("fsdp", "expert"), None),
        P(("fsdp", "expert"), None),
        P(("fsdp", "expert"), None),
        P(("fsdp", "expert"), None),
        P(("fsdp", "expert")),
        P(("fsdp", "expert"), None),
        P("expert", "fsdp", None),
        P("expert", "fsdp", None),
        P("expert", "fsdp", None),
    )
    return jax.shard_map(
        per_device,
        mesh=mesh,
        in_specs=placed,
        out_specs=(
            P(None, ("fsdp", "expert"), None),
            P(None, ("fsdp", "expert"), None),
            P(("fsdp", "expert")),
            P(("fsdp", "expert"), None),
            P(("fsdp", "expert"), None),
            P(("fsdp", "expert"), None),
            P(("fsdp", "expert"), None),
            P(("fsdp", "expert")),
            P(("fsdp", "expert"), None),
            P("expert", "fsdp", None),
            P("expert", "fsdp", None),
            P("expert", "fsdp", None),
        ),
        check_vma=False,
    )
```
